32 devices in a mesh: vis: 16 (over z, y, x), chan: 2 (over core).
Axes of the slice: x: 2, y: 2, z: 4, core: 2. Of those that a mesh axis runs over, the one named last changes fastest.
Arguments:
- model: float32 [2, 64, 1024], P(None, 'vis', 'chan'), may hold values from -6 to 6
- kernels: float32 [2, 32, 8], replicated, may hold values from -1.5 to 1.5
- vis_data: float32 [2, 2, 131072], P(None, 'chan', 'vis'), may hold values from -6 to 6
- vis_weight: float32 [2, 131072], P('chan', 'vis'), may hold values from 0.2 to 2
- tile_list: int32 [2, 16, 16], P('chan', 'vis'), may hold values from 0 to 63, as said below
- vis_slot: int32 [2, 131072], P('chan', 'vis'), may hold values from 0 to 15
- vis_wplane: int32 [2, 131072], P('chan', 'vis'), may hold values from 0 to 31
- vis_offset: int32 [2, 2, 131072], P(None, 'chan', 'vis'), may hold values from 0 to 24
Outputs:
- model_step: float32 [2, 64, 1024], P(None, 'vis', 'chan')
- residual: float32 [2, 2, 131072], P(None, 'chan', 'vis')
The draws below stay inside these ranges and needn't reach their ends.
Inputs may be any that keep to these rules, and one draw needn't show every extreme that they name: `tile_list`: the 16 tiles of one block's list are different and have different owners t // 4.
All inputs are finite; a program needn't handle non-finite values.
Results may differ from the reference program's by a relative error of at most 0.0003.
Values sent between devices are 32-bit elements; how exact they have to be, the bound alone decides.
A program may use at most 64 MiB of HBM per device.

```python
import math
import jax
import jax.numpy as jnp
from jax import lax

TILE_SIDE = 32
CELLS = 1024
SUPPORT = 8
WPLANES = 32
NTERMS = 2
SLOTS = 16
TILE_DEV = 4
VIS_DEV = 8192
TILES = 64
NVIS = 131072
N_VIS = 16
N_CHAN = 2


def draw_tile_list(key, part):
    key_rank = jax.random.fold_in(key, 11)
    key_score = jax.random.fold_in(key, 12)
    key_within = jax.random.fold_in(key, 13)
    owners = jnp.arange(N_VIS, dtype=jnp.int32)
    order = jax.random.permutation(key_rank, N_VIS).astype(jnp.int32)
    rank = jnp.zeros((N_VIS,), jnp.int32).at[order].set(owners)
    favour = (N_VIS - rank) * 65536 // N_VIS
    noise = jax.random.randint(key_score, (N_CHAN, N_VIS, N_VIS), 0, 65536, dtype=jnp.int32)
    scores = (noise + favour[None, None, :]) * N_VIS + owners[None, None, :]
    first = (jnp.arange(N_CHAN, dtype=jnp.int32)[:, None, None] == 0) & (jnp.arange(N_VIS, dtype=jnp.int32)[None, :, None] == 0)
    forced = first & ((owners[None, None, :] == 0) | (owners[None, None, :] == N_VIS - 1))
    scores = scores + jnp.where(forced, jnp.int32(1 << 28), jnp.int32(0))
    picked = lax.top_k(scores, SLOTS)[1].astype(jnp.int32)
    within = jax.random.randint(key_within, (N_CHAN, N_VIS, SLOTS), 0, TILE_DEV, dtype=jnp.int32)
    first_slots = first[:, :, :1]
    within = jnp.where(first_slots & (picked == 0), jnp.int32(0), within)
    within = jnp.where(first_slots & (picked == N_VIS - 1), jnp.int32(TILE_DEV - 1), within)
    return picked * TILE_DEV + within


def place_ends(array, rng, least, top_value):
    dims = array.shape
    index_at = [jax.random.randint(jax.random.fold_in(rng, axis), (), 0, dims[axis]) for axis in range(len(dims))]
    array = array.at[tuple(index_at)].set(least)
    longest = dims.index(max(dims))
    index_at[longest] = (index_at[longest] + 1) % dims[longest]
    return array.at[tuple(index_at)].set(top_value)


def block_scale(stream_key, shape, shards, smallest, largest):
    level = 1.0
    for dim, shards_of in shards:
        steps = jax.random.uniform(jax.random.fold_in(jax.random.fold_in(stream_key, 6), dim), (shards_of,), jnp.float32, smallest / len(shards), largest / len(shards))
        level = level * jnp.repeat(jnp.exp(steps), shape[dim] // shards_of).reshape((-1,) + (1,) * (len(shape) - 1 - dim))
    return level


def centred(rng, dims, deviation, limit, split=(), kind=jnp.bfloat16):
    array = deviation * jax.random.normal(rng, dims, jnp.float32)
    if split:
        array = array * block_scale(rng, dims, split, -0.22, 0.18)
    return jnp.clip(array, -limit, limit).astype(kind)


def setup_inputs(seed: int = 0) -> dict:
    seeds = jax.random.split(jax.random.key(seed), 9)
    model = centred(seeds[0], (NTERMS, TILES, CELLS), 1.0, 6.0, ((1, 16), (2, 2)), jnp.float32)
    kernels = centred(seeds[1], (2, WPLANES, SUPPORT), 0.25, 1.5, (), jnp.float32)
    vis_data = centred(seeds[2], (2, N_CHAN, NVIS), 1.0, 6.0, ((1, 2), (2, 16)), jnp.float32)
    vis_weight = jnp.clip(jnp.exp(math.log(2.0) - 2.3025851 * jax.random.uniform(seeds[3], (N_CHAN, NVIS), jnp.float32) ** block_scale(seeds[3], (N_CHAN, NVIS), ((0, 2), (1, 16)), -0.2, 0.2)), 0.2, 2.0)
    tile_list = draw_tile_list(jax.random.fold_in(seeds[8], 71), 0)
    vis_slot = place_ends(jax.random.randint(seeds[5], (N_CHAN, NVIS), 0, SLOTS), jax.random.fold_in(seeds[5], 1), 0, SLOTS - 1).astype(jnp.int32)
    vis_wplane = place_ends(jax.random.randint(seeds[6], (N_CHAN, NVIS), 0, WPLANES), jax.random.fold_in(seeds[6], 1), 0, WPLANES - 1).astype(jnp.int32)
    vis_offset = place_ends(jax.random.randint(seeds[7], (2, N_CHAN, NVIS), 0, TILE_SIDE - SUPPORT + 1), jax.random.fold_in(seeds[7], 1), 0, TILE_SIDE - SUPPORT).astype(jnp.int32)
    return {"model": model, "kernels": kernels, "vis_data": vis_data, "vis_weight": vis_weight, "tile_list": tile_list, "vis_slot": vis_slot, "vis_wplane": vis_wplane, "vis_offset": vis_offset}


HIGH = lax.Precision.HIGHEST

def dft_tables(side):
    index = jnp.arange(side, dtype=jnp.int32)
    angle = 2.0 * math.pi / side * (index[:, None] * index[None, :] % side).astype(jnp.float32)
    scale = 1.0 / math.sqrt(side)
    return (jnp.cos(angle) * scale, -jnp.sin(angle) * scale)

def forward(images, cosine, sine):

    def triple(left, right):
        return jnp.einsum('pa,tab,bq->tqp', left, images, right, precision=HIGH)
    return (triple(cosine, cosine) - triple(sine, sine), triple(cosine, sine) + triple(sine, cosine))

def adjoint(part_re, part_im, cosine, sine):

    def triple(left, middle, right):
        return jnp.einsum('ap,tqp,qb->tab', left, middle, right, precision=HIGH)
    return triple(cosine, part_re, cosine) - triple(sine, part_re, sine) + triple(sine, part_im, cosine) + triple(cosine, part_im, sine)

def place(offset, taps, side):
    rows = jnp.arange(side, dtype=jnp.int32)[:, None]
    shift = rows - offset[None, :]
    total = jnp.zeros((side, offset.shape[0]), jnp.float32)
    for tap in range(taps.shape[0]):
        total = total + jnp.where(shift == tap, taps[tap][None, :], jnp.float32(0.0))
    return total

def crossed(left, right):
    return lax.dot_general(left, right, (((1,), (1,)), ((), ())), precision=HIGH)

def visibility_pass(grid_re, grid_im, slot, wplane, off_u, off_v, data_re, data_im, weight, kernels):
    slots, side = (grid_re.shape[0], grid_re.shape[1])
    planes = kernels.shape[1]
    picker = (jnp.arange(planes, dtype=jnp.int32)[:, None] == wplane[None, :]).astype(jnp.float32)
    taps_re = jnp.dot(kernels[0].T, picker, precision=HIGH)
    taps_im = jnp.dot(kernels[1].T, picker, precision=HIGH)
    a_re = place(off_u, taps_re, side)
    a_im = place(off_u, taps_im, side)
    b_re = place(off_v, taps_re, side)
    b_im = place(off_v, taps_im, side)
    flat_re = grid_re.reshape(slots * side, side)
    flat_im = grid_im.reshape(slots * side, side)
    y_re = jnp.dot(flat_re, a_re, precision=HIGH) - jnp.dot(flat_im, a_im, precision=HIGH)
    y_im = jnp.dot(flat_re, a_im, precision=HIGH) + jnp.dot(flat_im, a_re, precision=HIGH)
    y_re = y_re.reshape(slots, side, -1)
    y_im = y_im.reshape(slots, side, -1)
    owner = (jnp.arange(slots, dtype=jnp.int32)[:, None] == slot[None, :]).astype(jnp.float32)
    pred_re = lax.optimization_barrier(jnp.sum(owner * lax.optimization_barrier(jnp.sum(y_re * b_re[None] - y_im * b_im[None], axis=1)), axis=0))
    pred_im = lax.optimization_barrier(jnp.sum(owner * lax.optimization_barrier(jnp.sum(y_re * b_im[None] + y_im * b_re[None], axis=1)), axis=0))
    res_re = weight * (data_re - pred_re)
    res_im = weight * (data_im - pred_im)
    z_re = (owner[:, None, :] * (res_re * b_re + res_im * b_im)[None]).reshape(slots * side, -1)
    z_im = (owner[:, None, :] * (res_im * b_re - res_re * b_im)[None]).reshape(slots * side, -1)
    part_re = crossed(z_re, a_re) + crossed(z_im, a_im)
    part_im = crossed(z_im, a_re) - crossed(z_re, a_im)
    return (res_re, res_im, part_re.reshape(slots, side, side), part_im.reshape(slots, side, side))

def reference(model, kernels, vis_data, vis_weight, tile_list, vis_slot, vis_wplane, vis_offset):
    side = TILE_SIDE
    cells = side * side
    offsets_all = (jnp.arange(N_CHAN, dtype=jnp.float32) - 0.5 * (N_CHAN - 1)) / N_CHAN
    cosine, sine = dft_tables(side)
    count = VIS_DEV
    grad_zero = jnp.zeros((TILES, cells), jnp.float32)
    grad_one = jnp.zeros((TILES, cells), jnp.float32)
    collected = []
    for channel in range(N_CHAN):
        frequency = offsets_all[channel]
        image = (model[0] + frequency * model[1]).reshape(TILES, side, side)
        full_re, full_im = forward(image, cosine, sine)

        def one_block(carry, inputs):
            listed, slot, wplane, off_u, off_v, data_re, data_im, weight = inputs
            res_re, res_im, part_re, part_im = visibility_pass(full_re[listed], full_im[listed], slot, wplane, off_u, off_v, data_re, data_im, weight, kernels)
            return ((carry[0].at[listed].add(part_re), carry[1].at[listed].add(part_im)), (res_re, res_im))
        empty = jnp.zeros((TILES, side, side), jnp.float32)
        sequence = (tile_list[channel], vis_slot[channel].reshape(N_VIS, count), vis_wplane[channel].reshape(N_VIS, count), vis_offset[0, channel].reshape(N_VIS, count), vis_offset[1, channel].reshape(N_VIS, count), vis_data[0, channel].reshape(N_VIS, count), vis_data[1, channel].reshape(N_VIS, count), vis_weight[channel].reshape(N_VIS, count))
        (total_re, total_im), (out_re, out_im) = lax.scan(one_block, (empty, empty), sequence)
        dirty = adjoint(total_re, total_im, cosine, sine).reshape(TILES, cells)
        grad_zero = grad_zero + dirty
        grad_one = grad_one + frequency * dirty
        collected.append(jnp.stack([out_re.reshape(-1), out_im.reshape(-1)]))
    residual = jnp.stack(collected, axis=1)
    model_step = jnp.stack([grad_zero / N_CHAN, grad_one / jnp.sum(offsets_all * offsets_all)])
    return (model_step, residual)
```

```python
import functools
import math

import jax
import jax.numpy as jnp
import numpy as np
from jax import lax
from jax.experimental import pallas as pl
from jax.experimental.pallas import tpu as pltpu
from jax.sharding import PartitionSpec as P

TILE_SIDE = 32
LANES = 128
CHUNK = 512
HIGH = lax.Precision.HIGHEST
MESH = pl.DeviceIdType.MESH
F32 = jnp.float32
BF16 = jnp.bfloat16


def tables():
    side = TILE_SIDE
    index = np.arange(side)
    angle = 2.0 * math.pi / side * (index[:, None] * index[None, :] % side)
    cosine, sine = np.cos(angle) / math.sqrt(side), -np.sin(angle) / math.sqrt(side)
    lane = np.arange(LANES)
    rows = side * side // LANES
    per = LANES // side
    line = np.stack(
        [
            np.concatenate([m[:, per * r + lane // side] for m in (cosine, sine)], axis=0)
            for r in range(rows)
        ]
    )
    fre, fim = cosine[lane % side], sine[lane % side]
    g_re = np.concatenate([fre, -fim], axis=0)
    g_im = np.concatenate([fim, fre], axis=0)
    right = np.concatenate([np.tile(np.concatenate([g_re, -g_im], 1), (1, 4)),
                            np.tile(np.concatenate([g_im, g_re], 1), (1, 4))], axis=1)
    block_re = np.concatenate(
        [cosine, -sine, cosine, -sine, sine, cosine, sine, cosine], axis=0
    )
    block_im = np.concatenate(
        [-sine, -cosine, -sine, -cosine, cosine, -sine, cosine, -sine], axis=0
    )
    back = np.concatenate([np.tile(block_re, (1, per)), np.tile(block_im, (1, per))], axis=1)
    return line.astype(np.float32), right.astype(np.float32), back.astype(np.float32)


def split(values):
    high = values.astype(BF16)
    return high, (values - high.astype(F32)).astype(BF16)


def greet(vis, chan, n_vis, n_chan):
    barrier = pltpu.get_barrier_semaphore()

    def hello(k, carry):
        pl.semaphore_signal(
            barrier, inc=1, device_id=(lax.rem(vis + k, n_vis), chan), device_id_type=MESH
        )
        return carry

    lax.fori_loop(1, n_vis, hello, 0)
    for k in range(1, n_chan):
        pl.semaphore_signal(
            barrier, inc=1, device_id=(vis, lax.rem(chan + k, n_chan)), device_id_type=MESH
        )
    pl.semaphore_wait(barrier, n_vis - 1 + n_chan - 1)


def offset_of(channel, n_chan):
    return (channel.astype(F32) - 0.5 * (n_chan - 1)) / n_chan


def gather_kernel(n_vis, n_chan, model_ref, tiles_ref, send, stage, cs, cr, vs, vr):
    vis, chan = lax.axis_index("vis"), lax.axis_index("chan")
    tile_dev, piece = model_ref.shape[1], model_ref.shape[2]
    per = piece // LANES
    first, second = model_ref[0], model_ref[1]
    for k in range(1, n_chan):
        send[k] = first + offset_of(lax.rem(chan + k, n_chan), n_chan) * second
    stage[chan] = first + offset_of(chan, n_chan) * second
    greet(vis, chan, n_vis, n_chan)
    swaps = []
    for k in range(1, n_chan):
        swap = pltpu.make_async_remote_copy(
            src_ref=send.at[k],
            dst_ref=stage.at[chan],
            send_sem=cs.at[k],
            recv_sem=cr.at[k],
            device_id=(vis, lax.rem(chan + k, n_chan)),
            device_id_type=MESH,
        )
        swap.start()
        swaps.append(swap)
    for swap in swaps:
        swap.wait()
    own = pl.ds(vis * tile_dev, tile_dev)
    for c in range(n_chan):
        part = stage[c]
        for j in range(per):
            tiles_ref[own, c * per + j, :] = part[:, LANES * j : LANES * (j + 1)]

    def copy(k):
        return pltpu.make_async_remote_copy(
            src_ref=tiles_ref.at[own],
            dst_ref=tiles_ref.at[own],
            send_sem=vs.at[k],
            recv_sem=vr.at[k],
            device_id=(lax.rem(vis + k, n_vis), chan),
            device_id_type=MESH,
        )

    def begin(k, carry):
        copy(k).start()
        return carry

    def finish(k, carry):
        copy(k).wait()
        return carry

    lax.fori_loop(1, n_vis, begin, 0)
    lax.fori_loop(1, n_vis, finish, 0)


def return_kernel(n_vis, n_chan, tiles_ref, step_ref, landed, send, stage, cs, cr, vs, vr):
    vis, chan = lax.axis_index("vis"), lax.axis_index("chan")
    tile_dev, piece = step_ref.shape[1], step_ref.shape[2]
    per = piece // LANES
    rows = per * n_chan
    greet(vis, chan, n_vis, n_chan)

    def copy(k):
        other = lax.rem(vis + k, n_vis)
        return pltpu.make_async_remote_copy(
            src_ref=tiles_ref.at[other],
            dst_ref=landed.at[k],
            send_sem=vs.at[k],
            recv_sem=vr.at[k],
            device_id=(other, chan),
            device_id_type=MESH,
        )

    def begin(k, carry):
        copy(k).start()
        return carry

    lax.fori_loop(1, n_vis, begin, 0)

    def added(total, block):
        return tuple(
            total[t] + block[:rows] * block[rows + t : rows + t + 1] for t in range(tile_dev)
        )

    def finish(k, total):
        copy(k).wait()
        return added(total, landed[k])

    zero = jnp.zeros((rows, LANES), F32)
    dirty = lax.fori_loop(1, n_vis, finish, added((zero,) * tile_dev, tiles_ref[vis]))
    for c in range(n_chan):
        for t in range(tile_dev):
            for j in range(per):
                row = c * per + j
                send[c, t : t + 1, LANES * j : LANES * (j + 1)] = dirty[t][row : row + 1]
    stage[chan] = send[chan]
    swaps = []
    for k in range(1, n_chan):
        other = lax.rem(chan + k, n_chan)
        swap = pltpu.make_async_remote_copy(
            src_ref=send.at[other],
            dst_ref=stage.at[chan],
            send_sem=cs.at[k],
            recv_sem=cr.at[k],
            device_id=(vis, other),
            device_id_type=MESH,
        )
        swap.start()
        swaps.append(swap)
    for swap in swaps:
        swap.wait()
    offsets = [(c - 0.5 * (n_chan - 1)) / n_chan for c in range(n_chan)]
    plain, sloped = stage[0], offsets[0] * stage[0]
    for c in range(1, n_chan):
        plain = plain + stage[c]
        sloped = sloped + offsets[c] * stage[c]
    step_ref[0] = plain / n_chan
    step_ref[1] = sloped / sum(x * x for x in offsets)


def block_kernel(
    listed_ref,
    tiles_ref,
    kernels_ref,
    data_ref,
    weight_ref,
    slot_ref,
    wplane_ref,
    offset_ref,
    line_ref,
    right_ref,
    back_ref,
    residual_ref,
    out_ref,
    w_ref,
    g_ref,
    y_ref,
    acc_ref,
):
    side = TILE_SIDE
    slots = listed_ref.shape[2]
    rows = tiles_ref.shape[1]
    tile_dev = tiles_ref.shape[0] // out_ref.shape[0]
    planes, taps = kernels_ref.shape[1], kernels_ref.shape[2]
    count = slot_ref.shape[1]
    size = y_ref.shape[1]

    for s in range(slots):
        tile = tiles_ref[listed_ref[0, 0, s]]
        w = line_ref[0] * tile[0:1]
        for r in range(1, rows):
            w = w + line_ref[r] * tile[r : r + 1]
        w_ref[side * s : side * (s + 1), :LANES] = w[:side]
        w_ref[side * s : side * (s + 1), LANES:] = w[side:]
    half = slots * side
    low_part = lax.broadcasted_iota(jnp.int32, (half, 2 * LANES), 1) >= LANES
    for i in range(2):
        grid = jnp.dot(
            w_ref[...],
            right_ref[:, 2 * LANES * i : 2 * LANES * (i + 1)],
            precision=HIGH,
            preferred_element_type=F32,
        )
        high = grid.astype(BF16).astype(F32)
        g_ref[half * i : half * (i + 1), :] = jnp.where(low_part, grid - high, high).astype(BF16)

    k_high, k_low = split(jnp.concatenate([kernels_ref[0], kernels_ref[1]], axis=1))
    acc_ref[...] = jnp.zeros_like(acc_ref)
    cell = lax.broadcasted_iota(jnp.int32, (side, size), 0)
    plane = lax.broadcasted_iota(jnp.int32, (planes, size), 0)

    def body(step, carry):
        here = pl.ds(pl.multiple_of(step * size, size), size)
        slot = slot_ref[:, here]
        picker = jnp.where(plane == wplane_ref[:, here], 1.0, 0.0).astype(BF16)
        contract = (((0,), (0,)), ((), ()))
        tap = lax.dot_general(
            k_high, picker, contract, preferred_element_type=F32
        ) + lax.dot_general(k_low, picker, contract, preferred_element_type=F32)

        def place(offset):
            shift = cell - offset
            re = jnp.zeros((side, size), F32)
            im = jnp.zeros((side, size), F32)
            for t in range(taps):
                hit = shift == t
                re = jnp.where(hit, tap[t : t + 1], re)
                im = jnp.where(hit, tap[taps + t : taps + t + 1], im)
            return re, im

        a_re, a_im = place(offset_ref[0, :, here])
        b_re, b_im = place(offset_ref[1, :, here])
        b_high, b_low = split(jnp.concatenate([b_re, b_im], axis=0))
        both = jnp.concatenate([b_high, b_low], axis=0)
        y_ref[...] = jnp.dot(
            g_ref[...], jnp.concatenate([both, both], axis=0), preferred_element_type=F32
        )
        s_re = y_ref[:side]
        s_im = y_ref[half : half + side]
        for s in range(1, slots):
            hit = slot == s
            s_re = jnp.where(hit, y_ref[side * s : side * (s + 1)], s_re)
            s_im = jnp.where(hit, y_ref[half + side * s : half + side * (s + 1)], s_im)
        pred_re = jnp.sum(s_re * a_re - s_im * a_im, axis=0, keepdims=True)
        pred_im = jnp.sum(s_re * a_im + s_im * a_re, axis=0, keepdims=True)
        weight = weight_ref[:, here]
        res_re = weight * (data_ref[0, :, here] - pred_re)
        res_im = weight * (data_ref[1, :, here] - pred_im)
        residual_ref[0, :, here] = res_re
        residual_ref[1, :, here] = res_im
        z_high, z_low = split(
            jnp.concatenate(
                [res_re * a_re + res_im * a_im, res_im * a_re - res_re * a_im], axis=0
            )
        )
        z = jnp.concatenate([z_high, z_low], axis=0)
        group, parity = slot // 2, slot % 2
        left = jnp.concatenate(
            [z * jnp.where(group == g, 1.0, 0.0).astype(BF16) for g in range(slots // 2)], axis=0
        )
        right = jnp.concatenate(
            [both * jnp.where(parity == h, 1.0, 0.0).astype(BF16) for h in range(2)], axis=0
        )
        acc_ref[...] += lax.dot_general(
            left, right, (((1,), (1,)), ((), ())), preferred_element_type=F32
        )
        return carry

    lax.fori_loop(0, count // size, body, 0)

    for s in range(slots):
        g, h = s // 2, s % 2
        block = acc_ref[4 * side * g : 4 * side * (g + 1), LANES * h : LANES * (h + 1)]
        block = block[: 2 * side] + block[2 * side :]
        w_ref[side * s : side * (s + 1), :LANES] = block[:side]
        w_ref[side * s : side * (s + 1), LANES:] = block[side:]
    y_ref[:half, : 2 * LANES] = jnp.dot(
        w_ref[...], back_ref[...], precision=HIGH, preferred_element_type=F32
    )
    out_ref[...] = jnp.zeros_like(out_ref)
    marks = lax.broadcasted_iota(jnp.int32, (rows, LANES), 0)
    for s in range(slots):
        listed = listed_ref[0, 0, s]
        owner = listed // tile_dev
        u_re = y_ref[side * s : side * (s + 1), :LANES]
        u_im = y_ref[side * s : side * (s + 1), LANES : 2 * LANES]
        lines = [
            jnp.sum(line_ref[r, :side] * u_re + line_ref[r, side:] * u_im, axis=0, keepdims=True)
            for r in range(rows)
        ]
        out_ref[owner, :rows, :] = jnp.concatenate(lines, axis=0)
        out_ref[owner, rows:, :] = jnp.where(marks == listed % tile_dev, 1.0, 0.0)


VMEM = pl.BlockSpec(memory_space=pltpu.VMEM)
SMEM = pl.BlockSpec(memory_space=pltpu.SMEM)


def block_call(tiles, kernels, vis_data, vis_weight, tile_list, vis_slot, vis_wplane, vis_offset, n_vis):
    line, right, back = tables()
    rows = tiles.shape[1]
    slots = tile_list.shape[2]
    half = slots * TILE_SIDE
    count = vis_slot.shape[1]
    size = min(CHUNK, count)
    return pl.pallas_call(
        block_kernel,
        out_shape=(
            jax.ShapeDtypeStruct(vis_data.shape, F32),
            jax.ShapeDtypeStruct((n_vis, 2 * rows, LANES), F32),
        ),
        in_specs=[SMEM] + [VMEM] * 10,
        out_specs=(VMEM, VMEM),
        scratch_shapes=[
            pltpu.VMEM((half, 2 * LANES), F32),
            pltpu.VMEM((2 * half, 2 * LANES), BF16),
            pltpu.VMEM((2 * half, size), F32),
            pltpu.VMEM((slots // 2 * 4 * TILE_SIDE, 2 * LANES), F32),
        ],
        compiler_params=pltpu.CompilerParams(vmem_limit_bytes=40 * 1024 * 1024),
        name="block",
    )(
        tile_list, tiles, kernels, vis_data, vis_weight, vis_slot, vis_wplane, vis_offset,
        jnp.asarray(line), jnp.asarray(right), jnp.asarray(back),
    )


def shards(model, kernels, vis_data, vis_weight, tile_list, vis_slot, vis_wplane, vis_offset):
    n_vis, n_chan = lax.axis_size("vis"), lax.axis_size("chan")
    tile_dev, piece = model.shape[1], model.shape[2]
    rows = TILE_SIDE * TILE_SIDE // LANES

    def semaphores():
        return [
            pltpu.SemaphoreType.DMA((n_chan,)),
            pltpu.SemaphoreType.DMA((n_chan,)),
            pltpu.SemaphoreType.DMA((n_vis,)),
            pltpu.SemaphoreType.DMA((n_vis,)),
        ]

    pieces = pltpu.VMEM((n_chan, tile_dev, piece), F32)
    tiles = pl.pallas_call(
        functools.partial(gather_kernel, n_vis, n_chan),
        out_shape=jax.ShapeDtypeStruct((n_vis * tile_dev, rows, LANES), F32),
        in_specs=[VMEM],
        out_specs=VMEM,
        scratch_shapes=[pieces, pieces] + semaphores(),
        compiler_params=pltpu.CompilerParams(collective_id=0, has_side_effects=True),
        name="gather",
    )(model)
    residual, dirty = block_call(
        tiles, kernels, vis_data, vis_weight, tile_list, vis_slot, vis_wplane, vis_offset, n_vis
    )
    model_step = pl.pallas_call(
        functools.partial(return_kernel, n_vis, n_chan),
        out_shape=jax.ShapeDtypeStruct(model.shape, F32),
        in_specs=[VMEM],
        out_specs=VMEM,
        scratch_shapes=[pltpu.VMEM((n_vis, 2 * rows, LANES), F32), pieces, pieces] + semaphores(),
        compiler_params=pltpu.CompilerParams(collective_id=1, has_side_effects=True),
        name="back",
    )(dirty)
    return (model_step, residual)


def solution(mesh):
    placed = (
        P(None, "vis", "chan"),
        P(),
        P(None, "chan", "vis"),
        P("chan", "vis"),
        P("chan", "vis", None),
        P("chan", "vis"),
        P("chan", "vis"),
        P(None, "chan", "vis"),
    )
    return jax.shard_map(
        shards,
        mesh=mesh,
        in_specs=placed,
        out_specs=(P(None, "vis", "chan"), P(None, "chan", "vis")),
        check_vma=False,
    )
```

```python
import functools
import math

import jax
import jax.numpy as jnp
import numpy as np
from jax import lax
from jax.experimental import pallas as pl
from jax.experimental.pallas import tpu as pltpu
from jax.sharding import PartitionSpec as P

TILE_SIDE = 32
LANES = 128
CHUNK = 512
PARTS = 2
HIGH = lax.Precision.HIGHEST
MESH = pl.DeviceIdType.MESH
F32 = jnp.float32
BF16 = jnp.bfloat16


def tables():
    side = TILE_SIDE
    index = np.arange(side)
    angle = 2.0 * math.pi / side * (index[:, None] * index[None, :] % side)
    cosine, sine = np.cos(angle) / math.sqrt(side), -np.sin(angle) / math.sqrt(side)
    lane = np.arange(LANES)
    rows = side * side // LANES
    per = LANES // side
    line = np.stack(
        [
            np.concatenate([m[:, per * r + lane // side] for m in (cosine, sine)], axis=0)
            for r in range(rows)
        ]
    )
    fre, fim = cosine[lane % side], sine[lane % side]
    g_re = np.concatenate([fre, -fim], axis=0)
    g_im = np.concatenate([fim, fre], axis=0)
    right = np.concatenate([np.tile(np.concatenate([g_re, -g_im], 1), (1, 4)),
                            np.tile(np.concatenate([g_im, g_re], 1), (1, 4))], axis=1)
    block_re = np.concatenate(
        [cosine, -sine, cosine, -sine, sine, cosine, sine, cosine], axis=0
    )
    block_im = np.concatenate(
        [-sine, -cosine, -sine, -cosine, cosine, -sine, cosine, -sine], axis=0
    )
    back = np.concatenate([np.tile(block_re, (1, per)), np.tile(block_im, (1, per))], axis=1)
    return line.astype(np.float32), right.astype(np.float32), back.astype(np.float32)


def split(values):
    high = values.astype(BF16)
    return high, (values - high.astype(F32)).astype(BF16)


def greet(vis, chan, n_vis, n_chan):
    barrier = pltpu.get_barrier_semaphore()

    def hello(k, carry):
        pl.semaphore_signal(
            barrier, inc=1, device_id=(lax.rem(vis + k, n_vis), chan), device_id_type=MESH
        )
        return carry

    lax.fori_loop(1, n_vis, hello, 0)
    for k in range(1, n_chan):
        pl.semaphore_signal(
            barrier, inc=1, device_id=(vis, lax.rem(chan + k, n_chan)), device_id_type=MESH
        )
    pl.semaphore_wait(barrier, n_vis - 1 + n_chan - 1)


def offset_of(channel, n_chan):
    return (channel.astype(F32) - 0.5 * (n_chan - 1)) / n_chan


def gather_kernel(n_vis, n_chan, model_ref, tiles_ref, send, stage, cs, cr, vs, vr):
    vis, chan = lax.axis_index("vis"), lax.axis_index("chan")
    tile_dev, piece = model_ref.shape[1], model_ref.shape[2]
    per = piece // LANES
    first, second = model_ref[0], model_ref[1]
    for k in range(1, n_chan):
        send[k] = first + offset_of(lax.rem(chan + k, n_chan), n_chan) * second
    stage[chan] = first + offset_of(chan, n_chan) * second
    greet(vis, chan, n_vis, n_chan)
    swaps = []
    for k in range(1, n_chan):
        swap = pltpu.make_async_remote_copy(
            src_ref=send.at[k],
            dst_ref=stage.at[chan],
            send_sem=cs.at[k],
            recv_sem=cr.at[k],
            device_id=(vis, lax.rem(chan + k, n_chan)),
            device_id_type=MESH,
        )
        swap.start()
        swaps.append(swap)
    for swap in swaps:
        swap.wait()
    own = pl.ds(vis * tile_dev, tile_dev)
    for c in range(n_chan):
        part = stage[c]
        for j in range(per):
            tiles_ref[own, c * per + j, :] = part[:, LANES * j : LANES * (j + 1)]

    def copy(k):
        return pltpu.make_async_remote_copy(
            src_ref=tiles_ref.at[own],
            dst_ref=tiles_ref.at[own],
            send_sem=vs.at[k],
            recv_sem=vr.at[k],
            device_id=(lax.rem(vis + k, n_vis), chan),
            device_id_type=MESH,
        )

    def begin(k, carry):
        copy(k).start()
        return carry

    def finish(k, carry):
        copy(k).wait()
        return carry

    lax.fori_loop(1, n_vis, begin, 0)
    lax.fori_loop(1, n_vis, finish, 0)


def return_kernel(n_vis, n_chan, tiles_ref, stage, landed, send, cs, cr, vs, vr):
    vis, chan = lax.axis_index("vis"), lax.axis_index("chan")
    tile_dev, piece = stage.shape[1], stage.shape[2]
    per = piece // LANES
    rows = per * n_chan
    greet(vis, chan, n_vis, n_chan)

    def copy(k):
        other = lax.rem(vis + k, n_vis)
        return pltpu.make_async_remote_copy(
            src_ref=tiles_ref.at[other],
            dst_ref=landed.at[k],
            send_sem=vs.at[k],
            recv_sem=vr.at[k],
            device_id=(other, chan),
            device_id_type=MESH,
        )

    def begin(k, carry):
        copy(k).start()
        return carry

    lax.fori_loop(1, n_vis, begin, 0)

    def added(total, block):
        return tuple(
            total[t] + block[:rows] * block[rows + t : rows + t + 1] for t in range(tile_dev)
        )

    def finish(k, total):
        copy(k).wait()
        return added(total, landed[k])

    zero = jnp.zeros((rows, LANES), F32)
    dirty = lax.fori_loop(1, n_vis, finish, added((zero,) * tile_dev, tiles_ref[vis]))
    for c in range(n_chan):
        for t in range(tile_dev):
            for j in range(per):
                row = c * per + j
                send[c, t : t + 1, LANES * j : LANES * (j + 1)] = dirty[t][row : row + 1]
    stage[chan] = send[chan]
    swaps = []
    for k in range(1, n_chan):
        other = lax.rem(chan + k, n_chan)
        swap = pltpu.make_async_remote_copy(
            src_ref=send.at[other],
            dst_ref=stage.at[chan],
            send_sem=cs.at[k],
            recv_sem=cr.at[k],
            device_id=(vis, other),
            device_id_type=MESH,
        )
        swap.start()
        swaps.append(swap)
    for swap in swaps:
        swap.wait()


def block_kernel(
    listed_ref,
    tiles_ref,
    kernels_ref,
    *rest,
):
    sources, rest = rest[:8], rest[8:]
    residual_ref, out_ref, w_ref, g_ref, y_ref, acc_ref, z_ref, b_ref = rest[:8]
    held, sems = rest[8:16], rest[16]
    fetches = [
        pltpu.make_async_copy(source, target, sems.at[i])
        for i, (source, target) in enumerate(zip(sources, held))
    ]
    for fetch in fetches:
        fetch.start()
    line_ref, right_ref, data_ref, weight_ref, slot_ref, wplane_ref, offset_ref, back_ref = held
    side = TILE_SIDE
    slots = listed_ref.shape[2]
    rows = tiles_ref.shape[1]
    tile_dev = tiles_ref.shape[0] // out_ref.shape[0]
    planes, taps = kernels_ref.shape[1], kernels_ref.shape[2]
    count = slot_ref.shape[1]
    size = y_ref.shape[2]

    fetches[0].wait()
    fetches[1].wait()
    for s in range(slots):
        tile = tiles_ref[listed_ref[0, 0, s]]
        w = line_ref[0] * tile[0:1]
        for r in range(1, rows):
            w = w + line_ref[r] * tile[r : r + 1]
        w_ref[side * s : side * (s + 1), :LANES] = w[:side]
        w_ref[side * s : side * (s + 1), LANES:] = w[side:]
    half = slots * side
    low_part = lax.broadcasted_iota(jnp.int32, (half, 2 * LANES), 1) >= LANES
    for i in range(2):
        grid = jnp.dot(
            w_ref[...],
            right_ref[:, 2 * LANES * i : 2 * LANES * (i + 1)],
            precision=HIGH,
            preferred_element_type=F32,
        )
        high = grid.astype(BF16).astype(F32)
        g_ref[half * i : half * (i + 1), :] = jnp.where(low_part, grid - high, high).astype(BF16)

    k_high, k_low = split(jnp.concatenate([kernels_ref[0], kernels_ref[1]], axis=1))
    acc_ref[...] = jnp.zeros_like(acc_ref)
    z_ref[...] = jnp.zeros_like(z_ref)
    b_ref[...] = jnp.zeros_like(b_ref)
    for fetch in fetches[2:]:
        fetch.wait()
    cell = lax.broadcasted_iota(jnp.int32, (side, size), 0)
    plane = lax.broadcasted_iota(jnp.int32, (planes, size), 0)

    def grid_held():
        acc_ref[...] += lax.dot_general(
            z_ref[...], b_ref[...], (((1,), (1,)), ((), ())), preferred_element_type=F32
        )

    def part(step, i):
        here = pl.ds(pl.multiple_of(step * (PARTS * size) + i * size, size), size)
        y = y_ref.at[i]
        slot = slot_ref[:, here]
        picker = jnp.where(plane == wplane_ref[:, here], 1.0, 0.0).astype(BF16)
        contract = (((0,), (0,)), ((), ()))
        tap = lax.dot_general(
            k_high, picker, contract, preferred_element_type=F32
        ) + lax.dot_general(k_low, picker, contract, preferred_element_type=F32)

        def place(offset):
            shift = cell - offset
            re = jnp.zeros((side, size), F32)
            im = jnp.zeros((side, size), F32)
            for t in range(taps):
                hit = shift == t
                re = jnp.where(hit, tap[t : t + 1], re)
                im = jnp.where(hit, tap[taps + t : taps + t + 1], im)
            return re, im

        a_re, a_im = place(offset_ref[0, :, here])
        b_re, b_im = place(offset_ref[1, :, here])
        b_high, b_low = split(jnp.concatenate([b_re, b_im], axis=0))
        both = jnp.concatenate([b_high, b_low], axis=0)
        y[...] = jnp.dot(
            g_ref[...], jnp.concatenate([both, both], axis=0), preferred_element_type=F32
        )
        s_re = y[:side]
        s_im = y[half : half + side]
        for s in range(1, slots):
            hit = slot == s
            s_re = jnp.where(hit, y[side * s : side * (s + 1)], s_re)
            s_im = jnp.where(hit, y[half + side * s : half + side * (s + 1)], s_im)
        pred_re = jnp.sum(s_re * a_re - s_im * a_im, axis=0, keepdims=True)
        pred_im = jnp.sum(s_re * a_im + s_im * a_re, axis=0, keepdims=True)
        weight = weight_ref[:, here]
        res_re = weight * (data_ref[0, :, here] - pred_re)
        res_im = weight * (data_ref[1, :, here] - pred_im)
        residual_ref[0, :, here] = res_re
        residual_ref[1, :, here] = res_im
        z_high, z_low = split(
            jnp.concatenate(
                [res_re * a_re + res_im * a_im, res_im * a_re - res_re * a_im], axis=0
            )
        )
        z = jnp.concatenate([z_high, z_low], axis=0)
        group, parity = slot // 2, slot % 2
        left = jnp.concatenate(
            [z * jnp.where(group == g, 1.0, 0.0).astype(BF16) for g in range(slots // 2)], axis=0
        )
        right = jnp.concatenate(
            [both * jnp.where(parity == h, 1.0, 0.0).astype(BF16) for h in range(2)], axis=0
        )
        return left, right

    def body(step, carry):
        grid_held()
        made = [part(step, i) for i in range(PARTS)]
        for i, (left, right) in enumerate(made):
            z_ref[:, size * i : size * (i + 1)] = left
            b_ref[:, size * i : size * (i + 1)] = right
        return carry

    lax.fori_loop(0, count // (PARTS * size), body, 0)
    grid_held()

    for s in range(slots):
        g, h = s // 2, s % 2
        block = acc_ref[4 * side * g : 4 * side * (g + 1), LANES * h : LANES * (h + 1)]
        block = block[: 2 * side] + block[2 * side :]
        w_ref[side * s : side * (s + 1), :LANES] = block[:side]
        w_ref[side * s : side * (s + 1), LANES:] = block[side:]
    y_ref[0, :half, : 2 * LANES] = jnp.dot(
        w_ref[...], back_ref[...], precision=HIGH, preferred_element_type=F32
    )
    out_ref[...] = jnp.zeros_like(out_ref)
    marks = lax.broadcasted_iota(jnp.int32, (rows, LANES), 0)
    for s in range(slots):
        listed = listed_ref[0, 0, s]
        owner = listed // tile_dev
        u_re = y_ref[0, side * s : side * (s + 1), :LANES]
        u_im = y_ref[0, side * s : side * (s + 1), LANES : 2 * LANES]
        lines = [
            jnp.sum(line_ref[r, :side] * u_re + line_ref[r, side:] * u_im, axis=0, keepdims=True)
            for r in range(rows)
        ]
        out_ref[owner, :rows, :] = jnp.concatenate(lines, axis=0)
        out_ref[owner, rows:, :] = jnp.where(marks == listed % tile_dev, 1.0, 0.0)


VMEM = pl.BlockSpec(memory_space=pltpu.VMEM)
SMEM = pl.BlockSpec(memory_space=pltpu.SMEM)


def block_call(tiles, kernels, vis_data, vis_weight, tile_list, vis_slot, vis_wplane, vis_offset, n_vis):
    line, right, back = tables()
    rows = tiles.shape[1]
    slots = tile_list.shape[2]
    half = slots * TILE_SIDE
    count = vis_slot.shape[1]
    size = CHUNK
    moved = (line, right, vis_data, vis_weight, vis_slot, vis_wplane, vis_offset, back)
    moved = tuple(jnp.asarray(array) for array in moved)
    return pl.pallas_call(
        block_kernel,
        out_shape=(
            jax.ShapeDtypeStruct(vis_data.shape, F32),
            jax.ShapeDtypeStruct((n_vis, 2 * rows, LANES), F32),
        ),
        in_specs=[SMEM, VMEM, VMEM] + [pl.BlockSpec(memory_space=pltpu.HBM)] * len(moved),
        out_specs=(VMEM, VMEM),
        scratch_shapes=[
            pltpu.VMEM((half, 2 * LANES), F32),
            pltpu.VMEM((2 * half, 2 * LANES), BF16),
            pltpu.VMEM((PARTS, 2 * half, size), F32),
            pltpu.VMEM((slots // 2 * 4 * TILE_SIDE, 2 * LANES), F32),
            pltpu.VMEM((slots // 2 * 4 * TILE_SIDE, PARTS * size), BF16),
            pltpu.VMEM((2 * LANES, PARTS * size), BF16),
        ]
        + [pltpu.VMEM(array.shape, array.dtype) for array in moved]
        + [pltpu.SemaphoreType.DMA((len(moved),))],
        compiler_params=pltpu.CompilerParams(vmem_limit_bytes=40 * 1024 * 1024),
        name="block",
    )(
        tile_list, tiles, kernels, *moved
    )


def shards(model, kernels, vis_data, vis_weight, tile_list, vis_slot, vis_wplane, vis_offset):
    n_vis, n_chan = lax.axis_size("vis"), lax.axis_size("chan")
    tile_dev, piece = model.shape[1], model.shape[2]
    rows = TILE_SIDE * TILE_SIDE // LANES

    def semaphores():
        return [
            pltpu.SemaphoreType.DMA((n_chan,)),
            pltpu.SemaphoreType.DMA((n_chan,)),
            pltpu.SemaphoreType.DMA((n_vis,)),
            pltpu.SemaphoreType.DMA((n_vis,)),
        ]

    pieces = pltpu.VMEM((n_chan, tile_dev, piece), F32)
    tiles = pl.pallas_call(
        functools.partial(gather_kernel, n_vis, n_chan),
        out_shape=jax.ShapeDtypeStruct((n_vis * tile_dev, rows, LANES), F32),
        in_specs=[VMEM],
        out_specs=VMEM,
        scratch_shapes=[pieces, pieces] + semaphores(),
        compiler_params=pltpu.CompilerParams(collective_id=0, has_side_effects=True),
        name="gather",
    )(model)
    residual, dirty = block_call(
        tiles, kernels, vis_data, vis_weight, tile_list, vis_slot, vis_wplane, vis_offset, n_vis
    )
    every = pl.pallas_call(
        functools.partial(return_kernel, n_vis, n_chan),
        out_shape=jax.ShapeDtypeStruct((n_chan, tile_dev, piece), F32),
        in_specs=[VMEM],
        out_specs=VMEM,
        scratch_shapes=[pltpu.VMEM((n_vis, 2 * rows, LANES), F32), pieces] + semaphores(),
        compiler_params=pltpu.CompilerParams(collective_id=1, has_side_effects=True),
        name="back",
    )(dirty)
    offsets = [(c - 0.5 * (n_chan - 1)) / n_chan for c in range(n_chan)]
    plain = sum(every[c] for c in range(n_chan)) / n_chan
    sloped = sum(offsets[c] * every[c] for c in range(n_chan)) / sum(x * x for x in offsets)
    return (jnp.stack([plain, sloped]), residual)


def solution(mesh):
    placed = (
        P(None, "vis", "chan"),
        P(),
        P(None, "chan", "vis"),
        P("chan", "vis"),
        P("chan", "vis", None),
        P("chan", "vis"),
        P("chan", "vis"),
        P(None, "chan", "vis"),
    )
    return jax.shard_map(
        shards,
        mesh=mesh,
        in_specs=placed,
        out_specs=(P(None, "vis", "chan"), P(None, "chan", "vis")),
        check_vma=False,
    )
```

```python
import functools
import math

import jax
import jax.numpy as jnp
import numpy as np
from jax import lax
from jax.experimental import pallas as pl
from jax.experimental.pallas import tpu as pltpu
from jax.sharding import PartitionSpec as P

TILE_SIDE = 32
LANES = 128
CHUNK = 512
PARTS = 2
HIGH = lax.Precision.HIGHEST
MESH = pl.DeviceIdType.MESH
F32 = jnp.float32
BF16 = jnp.bfloat16


def tables():
    side = TILE_SIDE
    index = np.arange(side)
    angle = 2.0 * math.pi / side * (index[:, None] * index[None, :] % side)
    cosine, sine = np.cos(angle) / math.sqrt(side), -np.sin(angle) / math.sqrt(side)
    lane = np.arange(LANES)
    rows = side * side // LANES
    per = LANES // side
    line = np.stack(
        [
            np.concatenate([m[:, per * r + lane // side] for m in (cosine, sine)], axis=0)
            for r in range(rows)
        ]
    )
    fre, fim = cosine[lane % side], sine[lane % side]
    g_re = np.concatenate([fre, -fim], axis=0)
    g_im = np.concatenate([fim, fre], axis=0)
    right = np.concatenate([np.tile(np.concatenate([g_re, -g_im], 1), (1, 4)),
                            np.tile(np.concatenate([g_im, g_re], 1), (1, 4))], axis=1)
    block_re = np.concatenate(
        [cosine, -sine, cosine, -sine, sine, cosine, sine, cosine], axis=0
    )
    block_im = np.concatenate(
        [-sine, -cosine, -sine, -cosine, cosine, -sine, cosine, -sine], axis=0
    )
    back = np.concatenate([np.tile(block_re, (1, per)), np.tile(block_im, (1, per))], axis=1)
    return line.astype(np.float32), right.astype(np.float32), back.astype(np.float32)


def split(values):
    high = values.astype(BF16)
    return high, (values - high.astype(F32)).astype(BF16)


def greet(vis, chan, n_vis, n_chan):
    barrier = pltpu.get_barrier_semaphore()

    def hello(k, carry):
        pl.semaphore_signal(
            barrier, inc=1, device_id=(lax.rem(vis + k, n_vis), chan), device_id_type=MESH
        )
        return carry

    lax.fori_loop(1, n_vis, hello, 0)
    for k in range(1, n_chan):
        pl.semaphore_signal(
            barrier, inc=1, device_id=(vis, lax.rem(chan + k, n_chan)), device_id_type=MESH
        )
    pl.semaphore_wait(barrier, n_vis - 1 + n_chan - 1)


def offset_of(channel, n_chan):
    return (channel.astype(F32) - 0.5 * (n_chan - 1)) / n_chan


def gather_kernel(n_vis, n_chan, model_ref, tiles_ref, send, stage, cs, cr, vs, vr):
    vis, chan = lax.axis_index("vis"), lax.axis_index("chan")
    tile_dev, piece = model_ref.shape[1], model_ref.shape[2]
    per = piece // LANES
    first, second = model_ref[0], model_ref[1]
    for k in range(1, n_chan):
        send[k] = first + offset_of(lax.rem(chan + k, n_chan), n_chan) * second
    stage[chan] = first + offset_of(chan, n_chan) * second
    greet(vis, chan, n_vis, n_chan)
    swaps = []
    for k in range(1, n_chan):
        swap = pltpu.make_async_remote_copy(
            src_ref=send.at[k],
            dst_ref=stage.at[chan],
            send_sem=cs.at[k],
            recv_sem=cr.at[k],
            device_id=(vis, lax.rem(chan + k, n_chan)),
            device_id_type=MESH,
        )
        swap.start()
        swaps.append(swap)
    for swap in swaps:
        swap.wait()
    own = pl.ds(vis * tile_dev, tile_dev)
    for c in range(n_chan):
        part = stage[c]
        for j in range(per):
            tiles_ref[own, c * per + j, :] = part[:, LANES * j : LANES * (j + 1)]

    def copy(k):
        return pltpu.make_async_remote_copy(
            src_ref=tiles_ref.at[own],
            dst_ref=tiles_ref.at[own],
            send_sem=vs.at[k],
            recv_sem=vr.at[k],
            device_id=(lax.rem(vis + k, n_vis), chan),
            device_id_type=MESH,
        )

    def begin(k, carry):
        copy(k).start()
        return carry

    def finish(k, carry):
        copy(k).wait()
        return carry

    lax.fori_loop(1, n_vis, begin, 0)
    lax.fori_loop(1, n_vis, finish, 0)


def return_kernel(n_vis, n_chan, tiles_ref, stage, landed, send, cs, cr, vs, vr):
    vis, chan = lax.axis_index("vis"), lax.axis_index("chan")
    tile_dev, piece = stage.shape[1], stage.shape[2]
    per = piece // LANES
    rows = per * n_chan
    greet(vis, chan, n_vis, n_chan)

    def copy(k):
        other = lax.rem(vis + k, n_vis)
        return pltpu.make_async_remote_copy(
            src_ref=tiles_ref.at[other],
            dst_ref=landed.at[k],
            send_sem=vs.at[k],
            recv_sem=vr.at[k],
            device_id=(other, chan),
            device_id_type=MESH,
        )

    def begin(k, carry):
        copy(k).start()
        return carry

    lax.fori_loop(1, n_vis, begin, 0)

    def added(total, block):
        return tuple(
            total[t] + block[:rows] * block[rows + t : rows + t + 1] for t in range(tile_dev)
        )

    def finish(k, total):
        copy(k).wait()
        return added(total, landed[k])

    zero = jnp.zeros((rows, LANES), F32)
    dirty = lax.fori_loop(1, n_vis, finish, added((zero,) * tile_dev, tiles_ref[vis]))
    for c in range(n_chan):
        for t in range(tile_dev):
            for j in range(per):
                row = c * per + j
                send[c, t : t + 1, LANES * j : LANES * (j + 1)] = dirty[t][row : row + 1]
    stage[chan] = send[chan]
    swaps = []
    for k in range(1, n_chan):
        other = lax.rem(chan + k, n_chan)
        swap = pltpu.make_async_remote_copy(
            src_ref=send.at[other],
            dst_ref=stage.at[chan],
            send_sem=cs.at[k],
            recv_sem=cr.at[k],
            device_id=(vis, other),
            device_id_type=MESH,
        )
        swap.start()
        swaps.append(swap)
    for swap in swaps:
        swap.wait()


def block_kernel(
    listed_ref,
    tiles_ref,
    kernels_ref,
    *rest,
):
    sources, rest = rest[:8], rest[8:]
    residual_ref, out_ref, w_ref, g_ref, y_ref, acc_ref, z_ref, b_ref = rest[:8]
    held, sems = rest[8:16], rest[16]
    fetches = [
        pltpu.make_async_copy(source, target, sems.at[i])
        for i, (source, target) in enumerate(zip(sources, held))
    ]
    for fetch in fetches:
        fetch.start()
    line_ref, right_ref, data_ref, weight_ref, slot_ref, wplane_ref, offset_ref, back_ref = held
    side = TILE_SIDE
    slots = listed_ref.shape[2]
    rows = tiles_ref.shape[1]
    tile_dev = tiles_ref.shape[0] // out_ref.shape[0]
    planes, taps = kernels_ref.shape[1], kernels_ref.shape[2]
    count = slot_ref.shape[1]
    size = y_ref.shape[2]

    fetches[0].wait()
    fetches[1].wait()
    for s in range(slots):
        tile = tiles_ref[listed_ref[0, 0, s]]
        w = line_ref[0] * tile[0:1]
        for r in range(1, rows):
            w = w + line_ref[r] * tile[r : r + 1]
        w_ref[side * s : side * (s + 1), :LANES] = w[:side]
        w_ref[side * s : side * (s + 1), LANES:] = w[side:]
    half = slots * side
    low_part = lax.broadcasted_iota(jnp.int32, (half, 2 * LANES), 1) >= LANES
    for i in range(2):
        grid = jnp.dot(
            w_ref[...],
            right_ref[:, 2 * LANES * i : 2 * LANES * (i + 1)],
            precision=HIGH,
            preferred_element_type=F32,
        )
        high = grid.astype(BF16).astype(F32)
        g_ref[half * i : half * (i + 1), :] = jnp.where(low_part, grid - high, high).astype(BF16)

    k_high, k_low = split(jnp.concatenate([kernels_ref[0], kernels_ref[1]], axis=1))
    acc_ref[...] = jnp.zeros_like(acc_ref)
    z_ref[...] = jnp.zeros_like(z_ref)
    b_ref[...] = jnp.zeros_like(b_ref)
    for fetch in fetches[2:]:
        fetch.wait()
    cell = lax.broadcasted_iota(jnp.int32, (side, size), 0)
    plane = lax.broadcasted_iota(jnp.int32, (planes, size), 0)

    def grid_held():
        acc_ref[...] += lax.dot_general(
            z_ref[...], b_ref[...], (((1,), (1,)), ((), ())), preferred_element_type=F32
        )

    def part(step, i):
        here = pl.ds(pl.multiple_of(step * (PARTS * size) + i * size, size), size)
        y = y_ref.at[i]
        slot = slot_ref[:, here]
        picker = jnp.where(plane == wplane_ref[:, here], 1.0, 0.0).astype(BF16)
        contract = (((0,), (0,)), ((), ()))
        tap = lax.dot_general(
            k_high, picker, contract, preferred_element_type=F32
        ) + lax.dot_general(k_low, picker, contract, preferred_element_type=F32)

        def place(offset):
            shift = cell - offset
            re = jnp.zeros((side, size), F32)
            im = jnp.zeros((side, size), F32)
            for t in range(taps):
                hit = shift == t
                re = jnp.where(hit, tap[t : t + 1], re)
                im = jnp.where(hit, tap[taps + t : taps + t + 1], im)
            return re, im

        a_re, a_im = place(offset_ref[0, :, here])
        b_re, b_im = place(offset_ref[1, :, here])
        b_high, b_low = split(jnp.concatenate([b_re, b_im], axis=0))
        both = jnp.concatenate([b_high, b_low], axis=0)
        y[...] = jnp.dot(
            g_ref[...], jnp.concatenate([both, both], axis=0), preferred_element_type=F32
        )
        s_re = y[:side]
        s_im = y[half : half + side]
        for s in range(1, slots):
            hit = slot == s
            s_re = jnp.where(hit, y[side * s : side * (s + 1)], s_re)
            s_im = jnp.where(hit, y[half + side * s : half + side * (s + 1)], s_im)
        pred_re = jnp.sum(s_re * a_re - s_im * a_im, axis=0, keepdims=True)
        pred_im = jnp.sum(s_re * a_im + s_im * a_re, axis=0, keepdims=True)
        weight = weight_ref[:, here]
        res_re = weight * (data_ref[0, :, here] - pred_re)
        res_im = weight * (data_ref[1, :, here] - pred_im)
        residual_ref[0, :, here] = res_re
        residual_ref[1, :, here] = res_im
        z_high, z_low = split(
            jnp.concatenate(
                [res_re * a_re + res_im * a_im, res_im * a_re - res_re * a_im], axis=0
            )
        )
        z = jnp.concatenate([z_high, z_low], axis=0)
        group, parity = slot // 2, slot % 2
        left = jnp.concatenate(
            [z * jnp.where(group == g, 1.0, 0.0).astype(BF16) for g in range(slots // 2)], axis=0
        )
        right = jnp.concatenate(
            [both * jnp.where(parity == h, 1.0, 0.0).astype(BF16) for h in range(2)], axis=0
        )
        return left, right

    def body(step, carry):
        grid_held()
        made = [part(step, i) for i in range(PARTS)]
        for i, (left, right) in enumerate(made):
            z_ref[:, size * i : size * (i + 1)] = left
            b_ref[:, size * i : size * (i + 1)] = right
        return carry

    lax.fori_loop(0, count // (PARTS * size), body, 0)
    grid_held()

    for s in range(slots):
        g, h = s // 2, s % 2
        block = acc_ref[4 * side * g : 4 * side * (g + 1), LANES * h : LANES * (h + 1)]
        block = block[: 2 * side] + block[2 * side :]
        w_ref[side * s : side * (s + 1), :LANES] = block[:side]
        w_ref[side * s : side * (s + 1), LANES:] = block[side:]
    y_ref[0, :half, : 2 * LANES] = jnp.dot(
        w_ref[...], back_ref[...], precision=HIGH, preferred_element_type=F32
    )
    out_ref[...] = jnp.zeros_like(out_ref)
    marks = lax.broadcasted_iota(jnp.int32, (rows, LANES), 0)
    for s in range(slots):
        listed = listed_ref[0, 0, s]
        owner = listed // tile_dev
        u_re = y_ref[0, side * s : side * (s + 1), :LANES]
        u_im = y_ref[0, side * s : side * (s + 1), LANES : 2 * LANES]
        lines = [
            jnp.sum(line_ref[r, :side] * u_re + line_ref[r, side:] * u_im, axis=0, keepdims=True)
            for r in range(rows)
        ]
        out_ref[owner, :rows, :] = jnp.concatenate(lines, axis=0)
        out_ref[owner, rows:, :] = jnp.where(marks == listed % tile_dev, 1.0, 0.0)


VMEM = pl.BlockSpec(memory_space=pltpu.VMEM)
SMEM = pl.BlockSpec(memory_space=pltpu.SMEM)


def block_call(tiles, kernels, vis_data, vis_weight, tile_list, vis_slot, vis_wplane, vis_offset, n_vis):
    line, right, back = tables()
    rows = tiles.shape[1]
    slots = tile_list.shape[2]
    half = slots * TILE_SIDE
    count = vis_slot.shape[1]
    size = CHUNK
    moved = (line, right, vis_data, vis_weight, vis_slot, vis_wplane, vis_offset, back)
    moved = tuple(jnp.asarray(array) for array in moved)
    return pl.pallas_call(
        block_kernel,
        out_shape=(
            jax.ShapeDtypeStruct(vis_data.shape, F32),
            jax.ShapeDtypeStruct((n_vis, 2 * rows, LANES), F32),
        ),
        in_specs=[SMEM, VMEM, VMEM] + [pl.BlockSpec(memory_space=pltpu.HBM)] * len(moved),
        out_specs=(VMEM, VMEM),
        scratch_shapes=[
            pltpu.VMEM((half, 2 * LANES), F32),
            pltpu.VMEM((2 * half, 2 * LANES), BF16),
            pltpu.VMEM((PARTS, 2 * half, size), F32),
            pltpu.VMEM((slots // 2 * 4 * TILE_SIDE, 2 * LANES), F32),
            pltpu.VMEM((slots // 2 * 4 * TILE_SIDE, PARTS * size), BF16),
            pltpu.VMEM((2 * LANES, PARTS * size), BF16),
        ]
        + [pltpu.VMEM(array.shape, array.dtype) for array in moved]
        + [pltpu.SemaphoreType.DMA((len(moved),))],
        compiler_params=pltpu.CompilerParams(vmem_limit_bytes=63 * 1024 * 1024),
        name="block",
    )(
        tile_list, tiles, kernels, *moved
    )


def shards(model, kernels, vis_data, vis_weight, tile_list, vis_slot, vis_wplane, vis_offset):
    n_vis, n_chan = lax.axis_size("vis"), lax.axis_size("chan")
    tile_dev, piece = model.shape[1], model.shape[2]
    rows = TILE_SIDE * TILE_SIDE // LANES

    def semaphores():
        return [
            pltpu.SemaphoreType.DMA((n_chan,)),
            pltpu.SemaphoreType.DMA((n_chan,)),
            pltpu.SemaphoreType.DMA((n_vis,)),
            pltpu.SemaphoreType.DMA((n_vis,)),
        ]

    pieces = pltpu.VMEM((n_chan, tile_dev, piece), F32)
    tiles = pl.pallas_call(
        functools.partial(gather_kernel, n_vis, n_chan),
        out_shape=jax.ShapeDtypeStruct((n_vis * tile_dev, rows, LANES), F32),
        in_specs=[VMEM],
        out_specs=VMEM,
        scratch_shapes=[pieces, pieces] + semaphores(),
        compiler_params=pltpu.CompilerParams(collective_id=0, has_side_effects=True),
        name="gather",
    )(model)
    residual, dirty = block_call(
        tiles, kernels, vis_data, vis_weight, tile_list, vis_slot, vis_wplane, vis_offset, n_vis
    )
    every = pl.pallas_call(
        functools.partial(return_kernel, n_vis, n_chan),
        out_shape=jax.ShapeDtypeStruct((n_chan, tile_dev, piece), F32),
        in_specs=[VMEM],
        out_specs=VMEM,
        scratch_shapes=[pltpu.VMEM((n_vis, 2 * rows, LANES), F32), pieces] + semaphores(),
        compiler_params=pltpu.CompilerParams(collective_id=1, has_side_effects=True),
        name="back",
    )(dirty)
    offsets = [(c - 0.5 * (n_chan - 1)) / n_chan for c in range(n_chan)]
    plain = sum(every[c] for c in range(n_chan)) / n_chan
    sloped = sum(offsets[c] * every[c] for c in range(n_chan)) / sum(x * x for x in offsets)
    return (jnp.stack([plain, sloped]), residual)


def solution(mesh):
    placed = (
        P(None, "vis", "chan"),
        P(),
        P(None, "chan", "vis"),
        P("chan", "vis"),
        P("chan", "vis", None),
        P("chan", "vis"),
        P("chan", "vis"),
        P(None, "chan", "vis"),
    )
    return jax.shard_map(
        shards,
        mesh=mesh,
        in_specs=placed,
        out_specs=(P(None, "vis", "chan"), P(None, "chan", "vis")),
        check_vma=False,
    )
```

```python
import functools
import math

import jax
import jax.numpy as jnp
import numpy as np
from jax import lax
from jax.experimental import pallas as pl
from jax.experimental.pallas import tpu as pltpu
from jax.sharding import PartitionSpec as P

TILE_SIDE = 32
LANES = 128
CHUNK = 512
PARTS = 2
HIGH = lax.Precision.HIGHEST
MESH = pl.DeviceIdType.MESH
F32 = jnp.float32
BF16 = jnp.bfloat16


def tables():
    side = TILE_SIDE
    index = np.arange(side)
    angle = 2.0 * math.pi / side * (index[:, None] * index[None, :] % side)
    cosine, sine = np.cos(angle) / math.sqrt(side), -np.sin(angle) / math.sqrt(side)
    lane = np.arange(LANES)
    rows = side * side // LANES
    per = LANES // side
    line = np.stack(
        [
            np.concatenate([m[:, per * r + lane // side] for m in (cosine, sine)], axis=0)
            for r in range(rows)
        ]
    )
    fre, fim = cosine[lane % side], sine[lane % side]
    g_re = np.concatenate([fre, -fim], axis=0)
    g_im = np.concatenate([fim, fre], axis=0)
    right = np.concatenate([np.tile(np.concatenate([g_re, -g_im], 1), (1, 4)),
                            np.tile(np.concatenate([g_im, g_re], 1), (1, 4))], axis=1)
    block_re = np.concatenate(
        [cosine, -sine, cosine, -sine, sine, cosine, sine, cosine], axis=0
    )
    block_im = np.concatenate(
        [-sine, -cosine, -sine, -cosine, cosine, -sine, cosine, -sine], axis=0
    )
    back = np.concatenate([np.tile(block_re, (1, per)), np.tile(block_im, (1, per))], axis=1)
    return line.astype(np.float32), right.astype(np.float32), back.astype(np.float32)


def split(values):
    high = values.astype(BF16)
    return high, (values - high.astype(F32)).astype(BF16)


def greet(vis, chan, n_vis, n_chan):
    barrier = pltpu.get_barrier_semaphore()

    def hello(k, carry):
        pl.semaphore_signal(
            barrier, inc=1, device_id=(lax.rem(vis + k, n_vis), chan), device_id_type=MESH
        )
        return carry

    lax.fori_loop(1, n_vis, hello, 0)
    for k in range(1, n_chan):
        pl.semaphore_signal(
            barrier, inc=1, device_id=(vis, lax.rem(chan + k, n_chan)), device_id_type=MESH
        )
    pl.semaphore_wait(barrier, n_vis - 1 + n_chan - 1)


def offset_of(channel, n_chan):
    return (channel.astype(F32) - 0.5 * (n_chan - 1)) / n_chan


def gather_kernel(n_vis, n_chan, model_ref, tiles_ref, send, stage, cs, cr, vs, vr):
    vis, chan = lax.axis_index("vis"), lax.axis_index("chan")
    tile_dev, piece = model_ref.shape[1], model_ref.shape[2]
    per = piece // LANES
    first, second = model_ref[0], model_ref[1]
    for k in range(1, n_chan):
        send[k] = first + offset_of(lax.rem(chan + k, n_chan), n_chan) * second
    stage[chan] = first + offset_of(chan, n_chan) * second
    greet(vis, chan, n_vis, n_chan)
    swaps = []
    for k in range(1, n_chan):
        swap = pltpu.make_async_remote_copy(
            src_ref=send.at[k],
            dst_ref=stage.at[chan],
            send_sem=cs.at[k],
            recv_sem=cr.at[k],
            device_id=(vis, lax.rem(chan + k, n_chan)),
            device_id_type=MESH,
        )
        swap.start()
        swaps.append(swap)
    for swap in swaps:
        swap.wait()
    own = pl.ds(vis * tile_dev, tile_dev)
    for c in range(n_chan):
        part = stage[c]
        for j in range(per):
            tiles_ref[own, c * per + j, :] = part[:, LANES * j : LANES * (j + 1)]

    def copy(k):
        return pltpu.make_async_remote_copy(
            src_ref=tiles_ref.at[own],
            dst_ref=tiles_ref.at[own],
            send_sem=vs.at[k],
            recv_sem=vr.at[k],
            device_id=(lax.rem(vis + k, n_vis), chan),
            device_id_type=MESH,
        )

    def begin(k, carry):
        copy(k).start()
        return carry

    def finish(k, carry):
        copy(k).wait()
        return carry

    lax.fori_loop(1, n_vis, begin, 0)
    lax.fori_loop(1, n_vis, finish, 0)


def return_kernel(n_vis, n_chan, tiles_ref, stage, landed, send, cs, cr, vs, vr):
    vis, chan = lax.axis_index("vis"), lax.axis_index("chan")
    tile_dev, piece = stage.shape[1], stage.shape[2]
    per = piece // LANES
    rows = per * n_chan
    greet(vis, chan, n_vis, n_chan)

    def copy(k):
        other = lax.rem(vis + k, n_vis)
        return pltpu.make_async_remote_copy(
            src_ref=tiles_ref.at[other],
            dst_ref=landed.at[k],
            send_sem=vs.at[k],
            recv_sem=vr.at[k],
            device_id=(other, chan),
            device_id_type=MESH,
        )

    def begin(k, carry):
        copy(k).start()
        return carry

    lax.fori_loop(1, n_vis, begin, 0)

    def added(total, block):
        return tuple(
            total[t] + block[:rows] * block[rows + t : rows + t + 1] for t in range(tile_dev)
        )

    def finish(k, total):
        copy(k).wait()
        return added(total, landed[k])

    zero = jnp.zeros((rows, LANES), F32)
    dirty = lax.fori_loop(1, n_vis, finish, added((zero,) * tile_dev, tiles_ref[vis]))
    for c in range(n_chan):
        for t in range(tile_dev):
            for j in range(per):
                row = c * per + j
                send[c, t : t + 1, LANES * j : LANES * (j + 1)] = dirty[t][row : row + 1]
    stage[chan] = send[chan]
    swaps = []
    for k in range(1, n_chan):
        other = lax.rem(chan + k, n_chan)
        swap = pltpu.make_async_remote_copy(
            src_ref=send.at[other],
            dst_ref=stage.at[chan],
            send_sem=cs.at[k],
            recv_sem=cr.at[k],
            device_id=(vis, other),
            device_id_type=MESH,
        )
        swap.start()
        swaps.append(swap)
    for swap in swaps:
        swap.wait()


def block_kernel(
    listed_ref,
    tiles_ref,
    kernels_ref,
    *rest,
):
    sources, rest = rest[:8], rest[8:]
    residual_ref, out_ref, w_ref, g_ref, y_ref, acc_ref, z_ref, b_ref = rest[:8]
    held, sems = rest[8:16], rest[16]
    fetches = [
        pltpu.make_async_copy(source, target, sems.at[i])
        for i, (source, target) in enumerate(zip(sources, held))
    ]
    for fetch in fetches:
        fetch.start()
    line_ref, right_ref, data_ref, weight_ref, slot_ref, wplane_ref, offset_ref, back_ref = held
    side = TILE_SIDE
    slots = listed_ref.shape[2]
    rows = tiles_ref.shape[1]
    tile_dev = tiles_ref.shape[0] // out_ref.shape[0]
    planes, taps = kernels_ref.shape[1], kernels_ref.shape[2]
    count = slot_ref.shape[1]
    size = y_ref.shape[2]

    fetches[0].wait()
    fetches[1].wait()
    for s in range(slots):
        tile = tiles_ref[listed_ref[0, 0, s]]
        w = line_ref[0] * tile[0:1]
        for r in range(1, rows):
            w = w + line_ref[r] * tile[r : r + 1]
        w_ref[side * s : side * (s + 1), :LANES] = w[:side]
        w_ref[side * s : side * (s + 1), LANES:] = w[side:]
    half = slots * side
    low_part = lax.broadcasted_iota(jnp.int32, (half, 2 * LANES), 1) >= LANES
    for i in range(2):
        grid = jnp.dot(
            w_ref[...],
            right_ref[:, 2 * LANES * i : 2 * LANES * (i + 1)],
            precision=HIGH,
            preferred_element_type=F32,
        )
        high = grid.astype(BF16).astype(F32)
        g_ref[half * i : half * (i + 1), :] = jnp.where(low_part, grid - high, high).astype(BF16)

    k_high, k_low = split(jnp.concatenate([kernels_ref[0], kernels_ref[1]], axis=1))
    acc_ref[...] = jnp.zeros_like(acc_ref)
    for fetch in fetches[2:]:
        fetch.wait()
    cell = lax.broadcasted_iota(jnp.int32, (side, size), 0)
    plane = lax.broadcasted_iota(jnp.int32, (planes, size), 0)

    def grid_held():
        acc_ref[...] += lax.dot_general(
            z_ref[...], b_ref[...], (((1,), (1,)), ((), ())), preferred_element_type=F32
        )

    def part(step, i):
        here = pl.ds(pl.multiple_of(step * (PARTS * size) + i * size, size), size)
        y = y_ref.at[i]
        slot = slot_ref[:, here]
        picker = jnp.where(plane == wplane_ref[:, here], 1.0, 0.0).astype(BF16)
        contract = (((0,), (0,)), ((), ()))
        tap = lax.dot_general(
            k_high, picker, contract, preferred_element_type=F32
        ) + lax.dot_general(k_low, picker, contract, preferred_element_type=F32)

        def place(offset):
            shift = cell - offset
            re = jnp.zeros((side, size), F32)
            im = jnp.zeros((side, size), F32)
            for t in range(taps):
                hit = shift == t
                re = jnp.where(hit, tap[t : t + 1], re)
                im = jnp.where(hit, tap[taps + t : taps + t + 1], im)
            return re, im

        a_re, a_im = place(offset_ref[0, :, here])
        b_re, b_im = place(offset_ref[1, :, here])
        b_high, b_low = split(jnp.concatenate([b_re, b_im], axis=0))
        both = jnp.concatenate([b_high, b_low], axis=0)
        y[...] = jnp.dot(
            g_ref[...], jnp.concatenate([both, both], axis=0), preferred_element_type=F32
        )
        s_re = y[:side]
        s_im = y[half : half + side]
        for s in range(1, slots):
            hit = slot == s
            s_re = jnp.where(hit, y[side * s : side * (s + 1)], s_re)
            s_im = jnp.where(hit, y[half + side * s : half + side * (s + 1)], s_im)
        pred_re = jnp.sum(s_re * a_re - s_im * a_im, axis=0, keepdims=True)
        pred_im = jnp.sum(s_re * a_im + s_im * a_re, axis=0, keepdims=True)
        weight = weight_ref[:, here]
        res_re = weight * (data_ref[0, :, here] - pred_re)
        res_im = weight * (data_ref[1, :, here] - pred_im)
        residual_ref[0, :, here] = res_re
        residual_ref[1, :, here] = res_im
        z_high, z_low = split(
            jnp.concatenate(
                [res_re * a_re + res_im * a_im, res_im * a_re - res_re * a_im], axis=0
            )
        )
        z = jnp.concatenate([z_high, z_low], axis=0)
        group, parity = slot // 2, slot % 2
        left = jnp.concatenate(
            [z * jnp.where(group == g, 1.0, 0.0).astype(BF16) for g in range(slots // 2)], axis=0
        )
        right = jnp.concatenate(
            [both * jnp.where(parity == h, 1.0, 0.0).astype(BF16) for h in range(2)], axis=0
        )
        return left, right

    def hold(step):
        made = [part(step, i) for i in range(PARTS)]
        for i, (left, right) in enumerate(made):
            z_ref[:, size * i : size * (i + 1)] = left
            b_ref[:, size * i : size * (i + 1)] = right

    def body(step, carry):
        grid_held()
        hold(step)
        return carry

    hold(0)

    lax.fori_loop(1, count // (PARTS * size), body, 0)
    grid_held()

    for s in range(slots):
        g, h = s // 2, s % 2
        block = acc_ref[4 * side * g : 4 * side * (g + 1), LANES * h : LANES * (h + 1)]
        block = block[: 2 * side] + block[2 * side :]
        w_ref[side * s : side * (s + 1), :LANES] = block[:side]
        w_ref[side * s : side * (s + 1), LANES:] = block[side:]
    y_ref[0, :half, : 2 * LANES] = jnp.dot(
        w_ref[...], back_ref[...], precision=HIGH, preferred_element_type=F32
    )
    out_ref[...] = jnp.zeros_like(out_ref)
    marks = lax.broadcasted_iota(jnp.int32, (rows, LANES), 0)
    for s in range(slots):
        listed = listed_ref[0, 0, s]
        owner = listed // tile_dev
        u_re = y_ref[0, side * s : side * (s + 1), :LANES]
        u_im = y_ref[0, side * s : side * (s + 1), LANES : 2 * LANES]
        lines = [
            jnp.sum(line_ref[r, :side] * u_re + line_ref[r, side:] * u_im, axis=0, keepdims=True)
            for r in range(rows)
        ]
        out_ref[owner, :rows, :] = jnp.concatenate(lines, axis=0)
        out_ref[owner, rows:, :] = jnp.where(marks == listed % tile_dev, 1.0, 0.0)


VMEM = pl.BlockSpec(memory_space=pltpu.VMEM)
SMEM = pl.BlockSpec(memory_space=pltpu.SMEM)


def block_call(tiles, kernels, vis_data, vis_weight, tile_list, vis_slot, vis_wplane, vis_offset, n_vis):
    line, right, back = tables()
    rows = tiles.shape[1]
    slots = tile_list.shape[2]
    half = slots * TILE_SIDE
    count = vis_slot.shape[1]
    size = CHUNK
    moved = (line, right, vis_data, vis_weight, vis_slot, vis_wplane, vis_offset, back)
    moved = tuple(jnp.asarray(array) for array in moved)
    return pl.pallas_call(
        block_kernel,
        out_shape=(
            jax.ShapeDtypeStruct(vis_data.shape, F32),
            jax.ShapeDtypeStruct((n_vis, 2 * rows, LANES), F32),
        ),
        in_specs=[SMEM, VMEM, VMEM] + [pl.BlockSpec(memory_space=pltpu.HBM)] * len(moved),
        out_specs=(VMEM, VMEM),
        scratch_shapes=[
            pltpu.VMEM((half, 2 * LANES), F32),
            pltpu.VMEM((2 * half, 2 * LANES), BF16),
            pltpu.VMEM((PARTS, 2 * half, size), F32),
            pltpu.VMEM((slots // 2 * 4 * TILE_SIDE, 2 * LANES), F32),
            pltpu.VMEM((slots // 2 * 4 * TILE_SIDE, PARTS * size), BF16),
            pltpu.VMEM((2 * LANES, PARTS * size), BF16),
        ]
        + [pltpu.VMEM(array.shape, array.dtype) for array in moved]
        + [pltpu.SemaphoreType.DMA((len(moved),))],
        compiler_params=pltpu.CompilerParams(vmem_limit_bytes=63 * 1024 * 1024),
        name="block",
    )(
        tile_list, tiles, kernels, *moved
    )


def shards(model, kernels, vis_data, vis_weight, tile_list, vis_slot, vis_wplane, vis_offset):
    n_vis, n_chan = lax.axis_size("vis"), lax.axis_size("chan")
    tile_dev, piece = model.shape[1], model.shape[2]
    rows = TILE_SIDE * TILE_SIDE // LANES

    def semaphores():
        return [
            pltpu.SemaphoreType.DMA((n_chan,)),
            pltpu.SemaphoreType.DMA((n_chan,)),
            pltpu.SemaphoreType.DMA((n_vis,)),
            pltpu.SemaphoreType.DMA((n_vis,)),
        ]

    pieces = pltpu.VMEM((n_chan, tile_dev, piece), F32)
    tiles = pl.pallas_call(
        functools.partial(gather_kernel, n_vis, n_chan),
        out_shape=jax.ShapeDtypeStruct((n_vis * tile_dev, rows, LANES), F32),
        in_specs=[VMEM],
        out_specs=VMEM,
        scratch_shapes=[pieces, pieces] + semaphores(),
        compiler_params=pltpu.CompilerParams(collective_id=0, has_side_effects=True),
        name="gather",
    )(model)
    residual, dirty = block_call(
        tiles, kernels, vis_data, vis_weight, tile_list, vis_slot, vis_wplane, vis_offset, n_vis
    )
    every = pl.pallas_call(
        functools.partial(return_kernel, n_vis, n_chan),
        out_shape=jax.ShapeDtypeStruct((n_chan, tile_dev, piece), F32),
        in_specs=[VMEM],
        out_specs=VMEM,
        scratch_shapes=[pltpu.VMEM((n_vis, 2 * rows, LANES), F32), pieces] + semaphores(),
        compiler_params=pltpu.CompilerParams(collective_id=1, has_side_effects=True),
        name="back",
    )(dirty)
    offsets = [(c - 0.5 * (n_chan - 1)) / n_chan for c in range(n_chan)]
    plain = sum(every[c] for c in range(n_chan)) / n_chan
    sloped = sum(offsets[c] * every[c] for c in range(n_chan)) / sum(x * x for x in offsets)
    return (jnp.stack([plain, sloped]), residual)


def solution(mesh):
    placed = (
        P(None, "vis", "chan"),
        P(),
        P(None, "chan", "vis"),
        P("chan", "vis"),
        P("chan", "vis", None),
        P("chan", "vis"),
        P("chan", "vis"),
        P(None, "chan", "vis"),
    )
    return jax.shard_map(
        shards,
        mesh=mesh,
        in_specs=placed,
        out_specs=(P(None, "vis", "chan"), P(None, "chan", "vis")),
        check_vma=False,
    )
```
